32 devices in a mesh: grp: 2 (over y), section: 4 (over x, core), walk: 4 (over z).
Axes of the slice: x: 2, y: 2, z: 4, core: 2. Of those that a mesh axis runs over, the one named last changes fastest.
Arguments:
- states: bfloat16 [4, 4, 8, 128, 256], P('section', None, ('grp', 'walk')), parts along dimension 2, may hold values from -6 to 6
- pair_feats: bfloat16 [4, 8, 32, 16384], P(None, ('grp', 'walk')), parts along dimension 1, may hold values from -6 to 6
- top_cotangent: bfloat16 [4, 8, 128, 256], P(None, ('grp', 'walk')), parts along dimension 1, may hold values from -6 to 6
- w_key: bfloat16 [4, 256, 256], P('section', 'walk'), may hold values from -0.375 to 0.375
- w_msg: bfloat16 [4, 32, 256], P('section', None, 'walk'), may hold values from -1 to 1
- b_msg: float32 [4, 256], P('section'), may hold values from -3 to 3
- w_self: bfloat16 [4, 256, 256], P('section', 'walk'), may hold values from -0.375 to 0.375
- w_up: bfloat16 [4, 256, 256], P('section', 'walk'), may hold values from -0.375 to 0.375
- w_down: bfloat16 [4, 256, 256], P('section', 'walk'), may hold values from -0.375 to 0.375
- b_self: float32 [4, 256], P('section'), may hold values from -3 to 3
- spins: int32 [128], replicated, may hold values from 0 to 1
Outputs:
- dh_layers: bfloat16 [4, 4, 8, 128, 256], P('section', None, ('grp', 'walk')), parts along dimension 2
- grad_key: float32 [8, 256, 256], P(('grp', 'section'), 'walk'), parts along dimension 0
- grad_msg: float32 [8, 32, 256], P(('grp', 'section'), None, 'walk'), parts along dimension 0
- grad_bias_msg: float32 [8, 256], P(('grp', 'section'), 'walk'), parts along dimension 0
- grad_self: float32 [8, 256, 256], P(('grp', 'section'), 'walk'), parts along dimension 0
- grad_up: float32 [8, 256, 256], P(('grp', 'section'), 'walk'), parts along dimension 0
- grad_down: float32 [8, 256, 256], P(('grp', 'section'), 'walk'), parts along dimension 0
- grad_bias_self: float32 [8, 256], P(('grp', 'section'), 'walk'), parts along dimension 0
The draws below stay inside these ranges and needn't reach their ends.
There are 2 independent parts, one for each index of `grp`. The reference program is written for one: setup_inputs(seed, part) draws one part's arguments, and reference() takes and returns one part's arrays. A program takes and returns all parts, laid end to end along the dimension named above; an argument that names none is the same for every part. Nothing has to cross between parts.
Inputs may be any that keep to these rules, and one draw needn't show every extreme that they name: `spins`: each electron's spin label, 0 for up and 1 for down.
All inputs are finite; a program needn't handle non-finite values.
Results may differ from the reference program's by a relative error of at most 0.018.
Values may be sent and summed in bfloat16 or wider, within the bound.
A program may use at most 64 MiB of HBM per device.

```python
import jax
import jax.numpy as jnp
from jax import lax

D = 256
PAIR = 32
ELEC = 128
MB = 4
LAYERS = 4
WALKERS_MB = 4


def touch_ends(entries, key, low, top_value):
    longest = entries.shape.index(max(entries.shape))
    spots = []
    for shift in (0, 1):
        where = [jax.random.randint(jax.random.fold_in(key, axis), (), 0, length) for axis, length in enumerate(entries.shape)]
        where[longest] = (where[longest] + shift) % entries.shape[longest]
        spots.append(tuple(where))
    return entries.at[spots[0]].set(low).at[spots[1]].set(top_value)


def with_spikes(drawn, rng, source, target, shards_of, factor):
    owner, partner = [(jnp.arange(drawn.shape[position]) // (drawn.shape[position] // shards_of)).reshape([-1 if axis == position else 1 for axis in range(drawn.ndim)]) for position in (source, target)]
    chosen = jax.random.permutation(rng, shards_of)[partner]
    strong = (owner == chosen) | (owner == (partner + shards_of // 2) % shards_of)
    return jnp.where(strong, factor * drawn, drawn)


def block_levels(own_key, dims, shards, least, largest):
    loudness = 1.0
    for dim, parts in shards:
        steps = jax.random.uniform(jax.random.fold_in(jax.random.fold_in(own_key, 6), dim), (parts,), jnp.float32, least / len(shards), largest / len(shards))
        loudness = loudness * jnp.repeat(jnp.exp(steps), dims[dim] // parts).reshape((-1,) + (1,) * (len(dims) - 1 - dim))
    return loudness


def gaussian(stream_key, extent, scale, reach, shards=(), kind=jnp.bfloat16):
    values = scale * jax.random.normal(stream_key, extent, jnp.float32)
    if shards:
        values = values * block_levels(stream_key, extent, shards, -0.22, 0.18)
    return jnp.clip(values, -reach, reach).astype(kind)


def gaussian_with(own_key, dims, scale, reach, cuts, heavy, dtype=jnp.bfloat16):
    array = scale * jax.random.normal(own_key, dims, jnp.float32)
    if cuts:
        array = array * block_levels(own_key, dims, cuts, -0.22, 0.18)
    return jnp.clip(with_spikes(array, jax.random.fold_in(own_key, 3), *heavy), -reach, reach).astype(dtype)


def setup_inputs(seed: int = 0, part: int = 0) -> dict:
    key_of = jax.random.split(jax.random.key(seed), 12)
    own_keys = jax.random.split(jax.random.fold_in(key_of[11], part), 12)
    states = gaussian_with(own_keys[0], (LAYERS, MB, WALKERS_MB, ELEC, D), 1.0, 6.0, ((0, 4), (2, 4)), (2, 4, 4, 2.0))
    pair_feats = gaussian(own_keys[1], (MB, WALKERS_MB, PAIR, ELEC * ELEC), 1.0, 6.0, ((1, 4),))
    top_cotangent = gaussian_with(own_keys[2], (MB, WALKERS_MB, ELEC, D), 1.0, 6.0, ((1, 4),), (1, 3, 4, 2.0))
    w_key = gaussian(key_of[3], (LAYERS, D, D), D ** -0.5, 0.375, ((0, 4), (1, 4)))
    w_msg = gaussian(key_of[4], (LAYERS, PAIR, D), PAIR ** -0.5, 1.0, ((0, 4), (2, 4)))
    b_msg = gaussian(key_of[5], (LAYERS, D), 0.5, 3.0, ((0, 4),), jnp.float32)
    w_self = gaussian(key_of[6], (LAYERS, D, D), D ** -0.5, 0.375, ((0, 4), (1, 4)))
    w_up = gaussian(key_of[7], (LAYERS, D, D), D ** -0.5, 0.375, ((0, 4), (1, 4)))
    w_down = gaussian(key_of[8], (LAYERS, D, D), D ** -0.5, 0.375, ((0, 4), (1, 4)))
    b_self = gaussian(key_of[9], (LAYERS, D), 0.5, 3.0, ((0, 4),), jnp.float32)
    spins = touch_ends(jax.random.randint(key_of[10], (ELEC,), 0, 2), jax.random.fold_in(key_of[10], 1), 0, 1).astype(jnp.int32)
    return dict(states=states, pair_feats=pair_feats, top_cotangent=top_cotangent, w_key=w_key, w_msg=w_msg, b_msg=b_msg, w_self=w_self, w_up=w_up, w_down=w_down, b_self=b_self, spins=spins)


def walker_back(weights, spin_up, state, pairs, incoming):
    w_key, w_msg, b_msg, w_self, w_up, w_down, b_self = weights
    elec = state.shape[0]
    width = state.shape[1]
    keyed = jnp.dot(state, w_key, preferred_element_type=jnp.float32)
    pre_msg = jnp.dot(pairs.T, w_msg, preferred_element_type=jnp.float32).reshape(elec, elec, width)
    pre_msg = pre_msg + keyed[None, :, :] + b_msg[None, None, :]
    message = jnp.tanh(pre_msg).astype(jnp.bfloat16)
    spin_pair = jnp.stack([spin_up, 1.0 - spin_up], axis=1)
    spin_sums = (jnp.einsum("ijd,js->sid", message.astype(jnp.float32), spin_pair) * (2.0 / elec)).astype(jnp.bfloat16)
    sum_up = spin_sums[0]
    sum_down = spin_sums[1]
    zvalue = jnp.dot(state, w_self, preferred_element_type=jnp.float32)
    zvalue = zvalue + jnp.dot(sum_up, w_up, preferred_element_type=jnp.float32)
    zvalue = zvalue + jnp.dot(sum_down, w_down, preferred_element_type=jnp.float32) + b_self[None, :]
    tanh_z = jnp.tanh(zvalue)
    dzeta = (incoming.astype(jnp.float32) * (1.0 - tanh_z * tanh_z)).astype(jnp.bfloat16)
    dsum_up = jnp.dot(dzeta, w_up.T, preferred_element_type=jnp.float32)
    dsum_down = jnp.dot(dzeta, w_down.T, preferred_element_type=jnp.float32)
    msg_float = message.astype(jnp.float32)
    spread = dsum_up[:, None, :] * spin_up[None, :, None] + dsum_down[:, None, :] * (1.0 - spin_up)[None, :, None]
    dpre = ((2.0 / elec) * spread * (1.0 - msg_float * msg_float)).astype(jnp.bfloat16)
    dkey = jnp.sum(dpre.astype(jnp.float32), axis=0).astype(jnp.bfloat16)
    dstate = incoming.astype(jnp.float32) + jnp.dot(dzeta, w_self.T, preferred_element_type=jnp.float32)
    dstate = (dstate + jnp.dot(dkey, w_key.T, preferred_element_type=jnp.float32)).astype(jnp.bfloat16)
    dpre_rows = dpre.reshape(elec * elec, width)
    terms = (
        jnp.dot(state.T, dkey, preferred_element_type=jnp.float32),
        jnp.dot(pairs, dpre_rows, preferred_element_type=jnp.float32),
        jnp.sum(dpre_rows.astype(jnp.float32), axis=0),
        jnp.dot(state.T, dzeta, preferred_element_type=jnp.float32),
        jnp.dot(sum_up.T, dzeta, preferred_element_type=jnp.float32),
        jnp.dot(sum_down.T, dzeta, preferred_element_type=jnp.float32),
        jnp.sum(dzeta.astype(jnp.float32), axis=0),
    )
    return dstate, terms


def reference(states, pair_feats, top_cotangent, w_key, w_msg, b_msg, w_self, w_up, w_down, b_self, spins):
    spin_up = (spins == 0).astype(jnp.float32)
    flat_pairs = pair_feats.reshape(-1, PAIR, ELEC * ELEC)
    carried = top_cotangent.reshape(-1, ELEC, D)
    layer_cots = []
    layer_grads = []
    for layer in range(LAYERS - 1, -1, -1):
        weights = (w_key[layer], w_msg[layer], b_msg[layer], w_self[layer], w_up[layer], w_down[layer], b_self[layer])
        flat_states = states[layer].reshape(-1, ELEC, D)

        def step(totals, items, weights=weights):
            state, pairs, incoming = items
            dstate, terms = walker_back(weights, spin_up, state, pairs, incoming)
            return tuple(total + term for total, term in zip(totals, terms)), dstate

        init = (
            jnp.zeros((D, D), jnp.float32),
            jnp.zeros((PAIR, D), jnp.float32),
            jnp.zeros((D,), jnp.float32),
            jnp.zeros((D, D), jnp.float32),
            jnp.zeros((D, D), jnp.float32),
            jnp.zeros((D, D), jnp.float32),
            jnp.zeros((D,), jnp.float32),
        )
        totals, carried = lax.scan(step, init, (flat_states, flat_pairs, carried))
        layer_cots.append(carried)
        layer_grads.append(totals)
    layer_cots = layer_cots[::-1]
    layer_grads = layer_grads[::-1]
    dh_layers = jnp.stack(layer_cots).reshape(LAYERS, MB, WALKERS_MB, ELEC, D)
    outs = []
    for which in range(7):
        outs.append(jnp.stack([grads[which] for grads in layer_grads]) / ELEC)
    return (dh_layers, outs[0], outs[1], outs[2], outs[3], outs[4], outs[5], outs[6])
```

```python
import functools

import jax
import jax.numpy as jnp
from jax import lax
from jax.experimental import pallas as pl
from jax.experimental.pallas import tpu as pltpu
from jax.sharding import PartitionSpec as P

F32 = jnp.float32
BF16 = jnp.bfloat16
MESH = pl.DeviceIdType.MESH


def dot(left, right):
    return jnp.dot(left, right, preferred_element_type=F32)


def dot_tn(left, right):
    return lax.dot_general(left, right, (((0,), (0,)), ((), ())), preferred_element_type=F32)


def dot_nt(left, right):
    return lax.dot_general(left, right, (((1,), (1,)), ((), ())), preferred_element_type=F32)


def join_rows(pieces):
    if pieces[0].shape[0] % 16:
        return jnp.concatenate([piece.astype(F32) for piece in pieces], axis=0).astype(BF16)
    return jnp.concatenate(pieces, axis=0)


def kernel(
    n_walk, n_section,
    states, pairs_hbm, top, wk, wm, bm, ws, wu, wd, bs, spins,
    dh, gk, gm, gbm, gs, gu, gd, gbs,
    slope, pairs, got_key, got_rest, got_msg, full_w, rhs, onehot, spin_rows, up_rows,
    sum_up_f, sum_down_f, sums, tz, arrived, dzs, dkeys, ds_up, ds_down,
    out_rest, in_rest, out_key, in_key, out_msg, in_msg,
    pair_sem, w_send, w_recv, p_send, p_recv, g_send, g_recv,
):
    walk = lax.axis_index("walk")
    section = lax.axis_index("section")
    micro, elec, width = states.shape
    pair_width = pairs.shape[1]
    rows = wk.shape[0]
    cols = wm.shape[1]
    scale = 2.0 / elec
    chunk = 8 * elec
    tile = 2 * elec
    chunks = elec // 8

    for w in range(micro):
        pltpu.make_async_copy(pairs_hbm.at[w], pairs.at[w], pair_sem.at[w]).start()

    peers = [lax.rem(walk + step, n_walk) for step in range(1, n_walk)]
    barrier = pltpu.get_barrier_semaphore()
    for peer in peers:
        pl.semaphore_signal(barrier, inc=1, device_id={"walk": peer}, device_id_type=MESH)
    above = lax.rem(section + 1, n_section)
    below = lax.rem(section + n_section - 1, n_section)
    pl.semaphore_signal(barrier, inc=1, device_id={"section": above}, device_id_type=MESH)
    pl.semaphore_signal(barrier, inc=1, device_id={"section": below}, device_id_type=MESH)

    got_key[walk] = wk[...]
    got_rest[walk, 0] = ws[...]
    got_rest[walk, 1] = wu[...]
    got_rest[walk, 2] = wd[...]
    got_msg[walk] = jnp.concatenate([wm[...], jnp.zeros((pair_width, 128 - cols), BF16)], axis=1)

    pl.semaphore_wait(barrier, n_walk + 1)

    def weight_copy(kind, ref, step, slot):
        return pltpu.make_async_remote_copy(
            src_ref=ref.at[slot], dst_ref=ref.at[slot],
            send_sem=w_send.at[kind, step], recv_sem=w_recv.at[kind, slot],
            device_id={"walk": peers[step]}, device_id_type=MESH,
        )

    kinds = ((0, got_key), (1, got_msg), (2, got_rest))
    for kind, ref in kinds:
        for step in range(n_walk - 1):
            weight_copy(kind, ref, step, walk).start()

    q = lax.broadcasted_iota(jnp.int32, (tile, elec), 0)
    j = lax.broadcasted_iota(jnp.int32, (tile, elec), 1)
    onehot[...] = jnp.where(lax.rem(q, elec) == j, 1.0, 0.0).astype(BF16)
    up = jnp.where(spins[...] == 0, 1.0, 0.0)
    up_both = jnp.concatenate([up, up], axis=1)
    r = lax.broadcasted_iota(jnp.int32, (16, tile), 0)
    q = lax.broadcasted_iota(jnp.int32, (16, tile), 1)
    chosen = jnp.where(r < 8, up_both, 1.0 - up_both)
    for k in range(4):
        spin_rows[k] = jnp.where(q // elec == lax.rem(r, 8) - 2 * k, chosen, 0.0).astype(BF16)
    up_column = jnp.transpose(jnp.broadcast_to(up, (elec, elec)))
    up_rows[...] = jnp.concatenate([up_column] * (width // elec), axis=1).astype(BF16)

    @pl.when(section == n_section - 1)
    def _():
        arrived[...] = top[...]

    for kind, ref in kinds[:2]:
        for step in range(n_walk - 1):
            weight_copy(kind, ref, step, peers[step]).wait_recv()
    full_w[0] = join_rows([got_key[k] for k in range(n_walk)])
    w_msg = jnp.concatenate([got_msg[k][:, :cols] for k in range(n_walk)], axis=1)
    for k in range(4):
        before = [jnp.zeros((k * pair_width, width), BF16)] if k else []
        after = [jnp.zeros(((3 - k) * pair_width, width), BF16)] if k < 3 else []
        rhs[k, 0:elec] = jnp.concatenate(before + [w_msg] + after, axis=0)

    def messages(w, _):
        pltpu.make_async_copy(pairs_hbm.at[w], pairs.at[w], pair_sem.at[w]).wait()
        keyed = (dot(states[w], full_w[0]) + bm[...]).astype(BF16)
        for k in range(4):
            rhs[k, elec:] = keyed

        def step(c, _):
            start = pl.multiple_of(c * chunk, chunk)
            block = pairs[w, :, pl.ds(start, chunk)]
            stacked = jnp.concatenate([block[:, k * tile:(k + 1) * tile] for k in range(4)], axis=0)
            left = jnp.concatenate([jnp.transpose(stacked), onehot[...]], axis=1)
            total = jnp.zeros((16, width), F32)
            for k in range(4):
                message = jnp.tanh(dot(left, rhs[k]).astype(BF16))
                slope[w, pl.ds(start + k * tile, tile), :] = 1.0 - message * message
                total = total + dot(spin_rows[k], message)
            at = pl.ds(pl.multiple_of(c * 8, 8), 8)
            sum_up_f[w, at, :] = total[:8] * scale
            sum_down_f[w, at, :] = total[8:] * scale
            return 0

        lax.fori_loop(0, chunks, step, 0)
        return 0

    lax.fori_loop(0, micro, messages, 0)

    for step in range(n_walk - 1):
        weight_copy(2, got_rest, step, peers[step]).wait_recv()
    for which in range(3):
        full_w[1 + which] = join_rows([got_rest[k, which] for k in range(n_walk)])
    flat = (micro * elec, width)
    sums[0] = sum_up_f[...].reshape(flat).astype(BF16)
    sums[1] = sum_down_f[...].reshape(flat).astype(BF16)
    h_all = states[...].reshape(flat)
    z = dot(h_all, full_w[1]) + dot(sums[0], full_w[2]) + dot(sums[1], full_w[3]) + bs[...]
    tanh_z = jnp.tanh(z)
    tz[...] = (1.0 - tanh_z * tanh_z).reshape(micro, elec, width)

    def down(w):
        return pltpu.make_async_remote_copy(
            src_ref=dh.at[w], dst_ref=arrived.at[w],
            send_sem=p_send.at[w], recv_sem=p_recv.at[w],
            device_id={"section": below}, device_id_type=MESH,
        )

    def grad_copy(kind, out, into, step, target, slot):
        return pltpu.make_async_remote_copy(
            src_ref=out.at[target], dst_ref=into.at[slot],
            send_sem=g_send.at[kind, step], recv_sem=g_recv.at[kind, slot],
            device_id={"walk": peers[step]}, device_id_type=MESH,
        )

    def walker(w, carry):
        grad_msg, bias_msg, bias_self = carry

        @pl.when(section < n_section - 1)
        def _():
            down(w).wait_recv()

        incoming = arrived[w].astype(F32)
        dz = (incoming * tz[w]).astype(BF16)
        here = pl.ds(pl.multiple_of(w * elec, elec), elec)
        dzs[here, :] = dz
        ds_up[...] = dot_nt(dz, full_w[2]) * scale
        ds_down[...] = dot_nt(dz, full_w[3]) * scale

        def step(c, carry):
            dkey, grad = carry
            at = pl.ds(pl.multiple_of(c * 8, 8), 8)
            row_up = ds_up[at, :]
            row_down = ds_down[at, :]
            start = pl.multiple_of(c * chunk, chunk)
            parts = []
            for i in range(8):
                one_up = jnp.broadcast_to(row_up[i:i + 1], (elec, width)).astype(BF16)
                one_down = jnp.broadcast_to(row_down[i:i + 1], (elec, width)).astype(BF16)
                spread = jnp.where(up_rows[...] > 0.5, one_up, one_down)
                parts.append(spread * slope[w, pl.ds(start + i * elec, elec), :])
            block = pairs[w, :, pl.ds(start, chunk)]
            for k in range(4):
                both = jnp.concatenate(parts[2 * k:2 * k + 2], axis=0)
                grad = grad + dot(block[:, k * tile:(k + 1) * tile], both)
            while len(parts) > 1:
                parts = [a + b for a, b in zip(parts[::2], parts[1::2])]
            return dkey + parts[0].astype(F32), grad

        dkey, grad_msg = lax.fori_loop(
            0, chunks, step, (jnp.zeros((elec, width), F32), grad_msg)
        )
        dkeys[here, :] = dkey.astype(BF16)
        out = incoming + dot_nt(dz, full_w[1]) + dot_nt(dkey.astype(BF16), full_w[0])
        dh[w] = out.astype(BF16)

        @pl.when(section > 0)
        def _():
            down(w).start()

        bias_msg = bias_msg + jnp.sum(dkey, axis=0, keepdims=True)
        bias_self = bias_self + jnp.sum(dz.astype(F32), axis=0, keepdims=True)
        return grad_msg, bias_msg, bias_self

    none = jnp.zeros((1, width), F32)
    grad_msg, bias_msg, bias_self = lax.fori_loop(
        0, micro, walker, (jnp.zeros((pair_width, width), F32), none, none)
    )

    lefts = (h_all, sums[0], sums[1])
    for which in range(3):
        grad = dot_tn(lefts[which], dzs[...])
        for k in range(n_walk):
            out_rest[k, which] = grad[k * rows:(k + 1) * rows].astype(BF16)
    for step in range(n_walk - 1):
        grad_copy(0, out_rest, in_rest, step, peers[step], walk).start()
    grad = dot_tn(h_all, dkeys[...])
    tail = jnp.concatenate(
        [grad_msg, bias_msg, bias_self, jnp.zeros((14, width), F32)], axis=0
    )
    for k in range(n_walk):
        out_key[k] = grad[k * rows:(k + 1) * rows].astype(BF16)
        part = tail[:, k * cols:(k + 1) * cols]
        out_msg[k] = jnp.concatenate(
            [part, jnp.zeros((tail.shape[0], 128 - cols), F32)], axis=1
        ).astype(BF16)
    for step in range(n_walk - 1):
        grad_copy(1, out_key, in_key, step, peers[step], walk).start()
        grad_copy(2, out_msg, in_msg, step, peers[step], walk).start()

    def collect(kind, out, into):
        total = out[walk].astype(F32)
        for step in range(n_walk - 1):
            grad_copy(kind, out, into, step, peers[step], peers[step]).wait_recv()
            total = total + into[peers[step]].astype(F32)
        return total * (1.0 / elec)

    rest = collect(0, out_rest, in_rest)
    gs[...] = rest[0]
    gu[...] = rest[1]
    gd[...] = rest[2]
    gk[...] = collect(1, out_key, in_key)
    last = collect(2, out_msg, in_msg)
    gm[...] = last[:pair_width, :cols]
    gbm[...] = last[pair_width:pair_width + 1, :cols]
    gbs[...] = last[pair_width + 1:pair_width + 2, :cols]

    for kind, ref in kinds:
        for step in range(n_walk - 1):
            weight_copy(kind, ref, step, walk).wait_send()
    for kind, out, into in ((0, out_rest, in_rest), (1, out_key, in_key), (2, out_msg, in_msg)):
        for step in range(n_walk - 1):
            grad_copy(kind, out, into, step, peers[step], walk).wait_send()

    @pl.when(section > 0)
    def _():
        for w in range(micro):
            down(w).wait_send()


def per_device(
    n_walk, n_section,
    states, pair_feats, top_cotangent, w_key, w_msg, b_msg, w_self, w_up, w_down, b_self, spins
):
    micro, walkers, elec, width = states.shape[1:]
    pair_width = pair_feats.shape[2]
    count = micro * walkers
    rows = w_key.shape[1]
    cols = w_msg.shape[2]
    tail = pair_width + 16
    vmem = pl.BlockSpec(memory_space=pltpu.VMEM)
    shape = jax.ShapeDtypeStruct
    outs = pl.pallas_call(
        functools.partial(kernel, n_walk, n_section),
        out_shape=(
            shape((count, elec, width), BF16),
            shape((rows, width), F32),
            shape((pair_width, cols), F32),
            shape((1, cols), F32),
            shape((rows, width), F32),
            shape((rows, width), F32),
            shape((rows, width), F32),
            shape((1, cols), F32),
        ),
        in_specs=[vmem, pl.BlockSpec(memory_space=pl.ANY)] + [vmem] * 9,
        out_specs=(vmem,) * 8,
        scratch_shapes=[
            pltpu.VMEM((count, elec * elec, width), BF16),
            pltpu.VMEM((count, pair_width, elec * elec), BF16),
            pltpu.VMEM((n_walk, rows, width), BF16),
            pltpu.VMEM((n_walk, 3, rows, width), BF16),
            pltpu.VMEM((n_walk, pair_width, 128), BF16),
            pltpu.VMEM((4, width, width), BF16),
            pltpu.VMEM((4, 2 * elec, width), BF16),
            pltpu.VMEM((2 * elec, elec), BF16),
            pltpu.VMEM((4, 16, 2 * elec), BF16),
            pltpu.VMEM((elec, width), BF16),
            pltpu.VMEM((count, elec, width), F32),
            pltpu.VMEM((count, elec, width), F32),
            pltpu.VMEM((2, count * elec, width), BF16),
            pltpu.VMEM((count, elec, width), F32),
            pltpu.VMEM((count, elec, width), BF16),
            pltpu.VMEM((count * elec, width), BF16),
            pltpu.VMEM((count * elec, width), BF16),
            pltpu.VMEM((elec, width), F32),
            pltpu.VMEM((elec, width), F32),
            pltpu.VMEM((n_walk, 3, rows, width), BF16),
            pltpu.VMEM((n_walk, 3, rows, width), BF16),
            pltpu.VMEM((n_walk, rows, width), BF16),
            pltpu.VMEM((n_walk, rows, width), BF16),
            pltpu.VMEM((n_walk, tail, 128), BF16),
            pltpu.VMEM((n_walk, tail, 128), BF16),
            pltpu.SemaphoreType.DMA((count,)),
            pltpu.SemaphoreType.DMA((3, n_walk)),
            pltpu.SemaphoreType.DMA((3, n_walk)),
            pltpu.SemaphoreType.DMA((count,)),
            pltpu.SemaphoreType.DMA((count,)),
            pltpu.SemaphoreType.DMA((3, n_walk)),
            pltpu.SemaphoreType.DMA((3, n_walk)),
        ],
        compiler_params=pltpu.CompilerParams(
            collective_id=0, has_side_effects=True, vmem_limit_bytes=58 * 1024 * 1024
        ),
    )(
        states[0].reshape(count, elec, width),
        pair_feats.reshape(count, pair_width, elec * elec),
        top_cotangent.reshape(count, elec, width),
        w_key[0], w_msg[0], b_msg, w_self[0], w_up[0], w_down[0], b_self,
        spins.reshape(1, elec),
    )
    dh, gk, gm, gbm, gs, gu, gd, gbs = outs
    return (
        dh.reshape(1, micro, walkers, elec, width),
        gk[None], gm[None], gbm, gs[None], gu[None], gd[None], gbs,
    )


def solution(mesh):
    in_specs = (
        P("section", None, ("grp", "walk"), None, None),
        P(None, ("grp", "walk"), None, None),
        P(None, ("grp", "walk"), None, None),
        P("section", "walk", None),
        P("section", None, "walk"),
        P("section", None),
        P("section", "walk", None),
        P("section", "walk", None),
        P("section", "walk", None),
        P("section", None),
        P(),
    )
    out_specs = (
        P("section", None, ("grp", "walk"), None, None),
        P(("grp", "section"), "walk", None),
        P(("grp", "section"), None, "walk"),
        P(("grp", "section"), "walk"),
        P(("grp", "section"), "walk", None),
        P(("grp", "section"), "walk", None),
        P(("grp", "section"), "walk", None),
        P(("grp", "section"), "walk"),
    )
    return jax.shard_map(
        functools.partial(per_device, mesh.shape["walk"], mesh.shape["section"]),
        mesh=mesh, in_specs=in_specs, out_specs=out_specs, check_vma=False,
    )
```

```python
import functools

import jax
import jax.numpy as jnp
from jax import lax
from jax.experimental import pallas as pl
from jax.experimental.pallas import tpu as pltpu
from jax.sharding import PartitionSpec as P

F32 = jnp.float32
BF16 = jnp.bfloat16
MESH = pl.DeviceIdType.MESH


def dot(left, right):
    return jnp.dot(left, right, preferred_element_type=F32)


def dot_tn(left, right):
    return lax.dot_general(left, right, (((0,), (0,)), ((), ())), preferred_element_type=F32)


def dot_nt(left, right):
    return lax.dot_general(left, right, (((1,), (1,)), ((), ())), preferred_element_type=F32)


def join_rows(pieces):
    if pieces[0].shape[0] % 16:
        return jnp.concatenate([piece.astype(F32) for piece in pieces], axis=0).astype(BF16)
    return jnp.concatenate(pieces, axis=0)


def fold(entries):
    while entries.shape[0] > 16:
        half = entries.shape[0] // 2
        entries = entries[:half] + entries[half:]
    return entries


def kernel(
    n_walk, n_section,
    states, pairs_hbm, top, wk, wm, bm, ws, wu, wd, bs, spins,
    dh, total_rest, total_key, total_msg,
    slope, pairs, got_key, got_rest, got_msg, full_w, rhs, onehot, fold_rows, up_rows,
    partial, sums, tz, arrived, dzs, dkeys, ds_up, ds_down,
    out_rest, in_rest, out_key, in_key, out_msg, in_msg,
    pair_sem, w_send, w_recv, p_send, p_recv, g_send, g_recv,
):
    walk = lax.axis_index("walk")
    section = lax.axis_index("section")
    micro, elec, width = states.shape
    pair_width = pairs.shape[1]
    rows = wk.shape[0]
    cols = wm.shape[1]
    scale = 2.0 / elec
    chunk = 8 * elec
    tile = 2 * elec
    chunks = elec // 8

    for w in range(micro):
        pltpu.make_async_copy(pairs_hbm.at[w], pairs.at[w], pair_sem.at[w]).start()

    peers = [lax.rem(walk + step, n_walk) for step in range(1, n_walk)]
    barrier = pltpu.get_barrier_semaphore()
    for peer in peers:
        pl.semaphore_signal(barrier, inc=1, device_id={"walk": peer}, device_id_type=MESH)
    above = lax.rem(section + 1, n_section)
    below = lax.rem(section + n_section - 1, n_section)
    pl.semaphore_signal(barrier, inc=1, device_id={"section": above}, device_id_type=MESH)
    pl.semaphore_signal(barrier, inc=1, device_id={"section": below}, device_id_type=MESH)

    got_key[walk] = wk[...]
    got_rest[walk, 0] = ws[...]
    got_rest[walk, 1] = wu[...]
    got_rest[walk, 2] = wd[...]
    got_msg[walk] = jnp.concatenate([wm[...], jnp.zeros((pair_width, 128 - cols), BF16)], axis=1)

    pl.semaphore_wait(barrier, n_walk + 1)

    def weight_copy(kind, ref, step, slot):
        return pltpu.make_async_remote_copy(
            src_ref=ref.at[slot], dst_ref=ref.at[slot],
            send_sem=w_send.at[kind, step], recv_sem=w_recv.at[kind, slot],
            device_id={"walk": peers[step]}, device_id_type=MESH,
        )

    kinds = ((0, got_key), (1, got_msg), (2, got_rest))
    for kind, ref in kinds:
        for step in range(n_walk - 1):
            weight_copy(kind, ref, step, walk).start()

    q = lax.broadcasted_iota(jnp.int32, (tile, elec), 0)
    j = lax.broadcasted_iota(jnp.int32, (tile, elec), 1)
    onehot[...] = jnp.where(lax.rem(q, elec) == j, 1.0, 0.0).astype(BF16)
    up = jnp.where(spins[...] == 0, 1.0, 0.0)
    r = lax.broadcasted_iota(jnp.int32, fold_rows.shape, 0)
    q = lax.broadcasted_iota(jnp.int32, fold_rows.shape, 1)
    fold_rows[...] = jnp.where(q // 16 == r, 1.0, 0.0).astype(BF16)
    up_column = jnp.transpose(jnp.broadcast_to(up, (elec, elec)))
    up_rows[...] = jnp.concatenate([up_column] * (width // elec), axis=1).astype(BF16)

    @pl.when(section == n_section - 1)
    def _():
        arrived[...] = top[...]

    for kind, ref in kinds[:2]:
        for step in range(n_walk - 1):
            weight_copy(kind, ref, step, peers[step]).wait_recv()
    full_w[0] = join_rows([got_key[k] for k in range(n_walk)])
    w_msg = jnp.concatenate([got_msg[k][:, :cols] for k in range(n_walk)], axis=1)
    for k in range(4):
        before = [jnp.zeros((k * pair_width, width), BF16)] if k else []
        after = [jnp.zeros(((3 - k) * pair_width, width), BF16)] if k < 3 else []
        rhs[k, 0:elec] = jnp.concatenate(before + [w_msg] + after, axis=0)

    def messages(w, _):
        pltpu.make_async_copy(pairs_hbm.at[w], pairs.at[w], pair_sem.at[w]).wait()
        keyed = (dot(states[w], full_w[0]) + bm[...]).astype(BF16)
        for k in range(4):
            rhs[k, elec:] = keyed

        def step(c, _):
            start = pl.multiple_of(c * chunk, chunk)
            block = pairs[w, :, pl.ds(start, chunk)]
            stacked = jnp.concatenate([block[:, k * tile:(k + 1) * tile] for k in range(4)], axis=0)
            left = jnp.concatenate([jnp.transpose(stacked), onehot[...]], axis=1)
            for k in range(4):
                message = jnp.tanh(dot(left, rhs[k]).astype(BF16))
                slope[w, pl.ds(start + k * tile, tile), :] = 1.0 - message * message
                for i in range(2):
                    one = message[i * elec:(i + 1) * elec]
                    at = pl.ds(pl.multiple_of(c * 128, 128) + (2 * k + i) * 16, 16)
                    partial[0, at, :] = fold(one)
                    partial[1, at, :] = fold(one * up_rows[...])
            return 0

        lax.fori_loop(0, chunks, step, 0, unroll=4)
        at = pl.ds(pl.multiple_of(w * elec, elec), elec)
        sum_both = dot(fold_rows[...], partial[0])
        sum_up = dot(fold_rows[...], partial[1])
        sums[0, at, :] = (sum_up * scale).astype(BF16)
        sums[1, at, :] = ((sum_both - sum_up) * scale).astype(BF16)
        return 0

    lax.fori_loop(0, micro, messages, 0)

    for step in range(n_walk - 1):
        weight_copy(2, got_rest, step, peers[step]).wait_recv()
    for which in range(3):
        full_w[1 + which] = join_rows([got_rest[k, which] for k in range(n_walk)])
    flat = (micro * elec, width)
    h_all = states[...].reshape(flat)
    z = dot(h_all, full_w[1]) + dot(sums[0], full_w[2]) + dot(sums[1], full_w[3]) + bs[...]
    tanh_z = jnp.tanh(z)
    tz[...] = (1.0 - tanh_z * tanh_z).reshape(micro, elec, width)

    def down(w):
        return pltpu.make_async_remote_copy(
            src_ref=dh.at[w], dst_ref=arrived.at[w],
            send_sem=p_send.at[w], recv_sem=p_recv.at[w],
            device_id={"section": below}, device_id_type=MESH,
        )

    def grad_copy(kind, out, into, step, target, slot):
        return pltpu.make_async_remote_copy(
            src_ref=out.at[target], dst_ref=into.at[slot],
            send_sem=g_send.at[kind, step], recv_sem=g_recv.at[kind, slot],
            device_id={"walk": peers[step]}, device_id_type=MESH,
        )

    def walker(w, carry):
        grad_msg, bias_msg, bias_self = carry

        @pl.when(section < n_section - 1)
        def _():
            down(w).wait_recv()

        incoming = arrived[w].astype(F32)
        dz = (incoming * tz[w]).astype(BF16)
        here = pl.ds(pl.multiple_of(w * elec, elec), elec)
        dzs[here, :] = dz
        ds_up[...] = dot_nt(dz, full_w[2]) * scale
        ds_down[...] = dot_nt(dz, full_w[3]) * scale

        def step(c, carry):
            dkey, grad = carry
            at = pl.ds(pl.multiple_of(c * 8, 8), 8)
            row_up = ds_up[at, :]
            row_down = ds_down[at, :]
            start = pl.multiple_of(c * chunk, chunk)
            parts = []
            for i in range(8):
                one_up = jnp.broadcast_to(row_up[i:i + 1], (elec, width)).astype(BF16)
                one_down = jnp.broadcast_to(row_down[i:i + 1], (elec, width)).astype(BF16)
                spread = jnp.where(up_rows[...] > 0.5, one_up, one_down)
                parts.append(spread * slope[w, pl.ds(start + i * elec, elec), :])
            block = pairs[w, :, pl.ds(start, chunk)]
            for k in range(4):
                both = jnp.concatenate(parts[2 * k:2 * k + 2], axis=0)
                grad = grad + dot(block[:, k * tile:(k + 1) * tile], both)
            while len(parts) > 1:
                parts = [a + b for a, b in zip(parts[::2], parts[1::2])]
            return dkey + parts[0].astype(F32), grad

        dkey, grad_msg = lax.fori_loop(
            0, chunks, step, (jnp.zeros((elec, width), F32), grad_msg), unroll=4
        )
        dkeys[here, :] = dkey.astype(BF16)
        out = incoming + dot_nt(dz, full_w[1]) + dot_nt(dkey.astype(BF16), full_w[0])
        dh[w] = out.astype(BF16)

        @pl.when(section > 0)
        def _():
            down(w).start()

        bias_msg = bias_msg + jnp.sum(dkey, axis=0, keepdims=True)
        bias_self = bias_self + jnp.sum(dz.astype(F32), axis=0, keepdims=True)
        return grad_msg, bias_msg, bias_self

    none = jnp.zeros((1, width), F32)
    grad_msg, bias_msg, bias_self = lax.fori_loop(
        0, micro, walker, (jnp.zeros((pair_width, width), F32), none, none)
    )

    lefts = (h_all, sums[0], sums[1])
    for which in range(3):
        grad = dot_tn(lefts[which], dzs[...])
        for k in range(n_walk):
            out_rest[k, which] = grad[k * rows:(k + 1) * rows].astype(BF16)
    for step in range(n_walk - 1):
        grad_copy(0, out_rest, in_rest, step, peers[step], walk).start()
    grad = dot_tn(h_all, dkeys[...])
    tail = jnp.concatenate(
        [grad_msg, bias_msg, bias_self, jnp.zeros((14, width), F32)], axis=0
    )
    for k in range(n_walk):
        out_key[k] = grad[k * rows:(k + 1) * rows].astype(BF16)
        part = tail[:, k * cols:(k + 1) * cols]
        out_msg[k] = jnp.concatenate(
            [part, jnp.zeros((tail.shape[0], 128 - cols), F32)], axis=1
        ).astype(BF16)
    for step in range(n_walk - 1):
        grad_copy(1, out_key, in_key, step, peers[step], walk).start()
        grad_copy(2, out_msg, in_msg, step, peers[step], walk).start()

    def collect(kind, out, into):
        total = out[walk].astype(F32)
        for step in range(n_walk - 1):
            grad_copy(kind, out, into, step, peers[step], peers[step]).wait_recv()
            total = total + into[peers[step]].astype(F32)
        return total * (1.0 / elec)

    total_rest[...] = collect(0, out_rest, in_rest)
    total_key[...] = collect(1, out_key, in_key)
    total_msg[...] = collect(2, out_msg, in_msg)

    for kind, ref in kinds:
        for step in range(n_walk - 1):
            weight_copy(kind, ref, step, walk).wait_send()
    for kind, out, into in ((0, out_rest, in_rest), (1, out_key, in_key), (2, out_msg, in_msg)):
        for step in range(n_walk - 1):
            grad_copy(kind, out, into, step, peers[step], walk).wait_send()

    @pl.when(section > 0)
    def _():
        for w in range(micro):
            down(w).wait_send()


def spread_out(
    dh_in, total_rest, total_key, total_msg, dh, gk, gm, gbm, gs, gu, gd, gbs
):
    pair_width, cols = gm.shape
    dh[...] = dh_in[...]
    gk[...] = total_key[...]
    gs[...] = total_rest[0]
    gu[...] = total_rest[1]
    gd[...] = total_rest[2]
    gm[...] = total_msg[:pair_width, :cols]
    gbm[...] = total_msg[pair_width:pair_width + 1, :cols]
    gbs[...] = total_msg[pair_width + 1:pair_width + 2, :cols]


def per_device(
    n_walk, n_section,
    states, pair_feats, top_cotangent, w_key, w_msg, b_msg, w_self, w_up, w_down, b_self, spins
):
    micro, walkers, elec, width = states.shape[1:]
    pair_width = pair_feats.shape[2]
    count = micro * walkers
    rows = w_key.shape[1]
    cols = w_msg.shape[2]
    tail = pair_width + 16
    vmem = pl.BlockSpec(memory_space=pltpu.VMEM)
    shape = jax.ShapeDtypeStruct
    raw = pl.pallas_call(
        functools.partial(kernel, n_walk, n_section),
        out_shape=(
            shape((count, elec, width), BF16),
            shape((3, rows, width), F32),
            shape((rows, width), F32),
            shape((tail, 128), F32),
        ),
        in_specs=[vmem, pl.BlockSpec(memory_space=pl.ANY)] + [vmem] * 9,
        out_specs=(vmem,) * 4,
        scratch_shapes=[
            pltpu.VMEM((count, elec * elec, width), BF16),
            pltpu.VMEM((count, pair_width, elec * elec), BF16),
            pltpu.VMEM((n_walk, rows, width), BF16),
            pltpu.VMEM((n_walk, 3, rows, width), BF16),
            pltpu.VMEM((n_walk, pair_width, 128), BF16),
            pltpu.VMEM((4, width, width), BF16),
            pltpu.VMEM((4, 2 * elec, width), BF16),
            pltpu.VMEM((2 * elec, elec), BF16),
            pltpu.VMEM((elec, 16 * elec), BF16),
            pltpu.VMEM((elec, width), BF16),
            pltpu.VMEM((2, 16 * elec, width), BF16),
            pltpu.VMEM((2, count * elec, width), BF16),
            pltpu.VMEM((count, elec, width), F32),
            pltpu.VMEM((count, elec, width), BF16),
            pltpu.VMEM((count * elec, width), BF16),
            pltpu.VMEM((count * elec, width), BF16),
            pltpu.VMEM((elec, width), F32),
            pltpu.VMEM((elec, width), F32),
            pltpu.VMEM((n_walk, 3, rows, width), BF16),
            pltpu.VMEM((n_walk, 3, rows, width), BF16),
            pltpu.VMEM((n_walk, rows, width), BF16),
            pltpu.VMEM((n_walk, rows, width), BF16),
            pltpu.VMEM((n_walk, tail, 128), BF16),
            pltpu.VMEM((n_walk, tail, 128), BF16),
            pltpu.SemaphoreType.DMA((count,)),
            pltpu.SemaphoreType.DMA((3, n_walk)),
            pltpu.SemaphoreType.DMA((3, n_walk)),
            pltpu.SemaphoreType.DMA((count,)),
            pltpu.SemaphoreType.DMA((count,)),
            pltpu.SemaphoreType.DMA((3, n_walk)),
            pltpu.SemaphoreType.DMA((3, n_walk)),
        ],
        compiler_params=pltpu.CompilerParams(
            collective_id=0, has_side_effects=True, vmem_limit_bytes=58 * 1024 * 1024
        ),
    )(
        states[0].reshape(count, elec, width),
        pair_feats.reshape(count, pair_width, elec * elec),
        top_cotangent.reshape(count, elec, width),
        w_key[0], w_msg[0], b_msg, w_self[0], w_up[0], w_down[0], b_self,
        spins.reshape(1, elec),
    )
    dh, gk, gm, gbm, gs, gu, gd, gbs = pl.pallas_call(
        spread_out,
        out_shape=(
            shape((count, elec, width), BF16),
            shape((rows, width), F32),
            shape((pair_width, cols), F32),
            shape((1, cols), F32),
            shape((rows, width), F32),
            shape((rows, width), F32),
            shape((rows, width), F32),
            shape((1, cols), F32),
        ),
        in_specs=[vmem] * 4,
        out_specs=(vmem,) * 8,
    )(*raw)
    return (
        dh.reshape(1, micro, walkers, elec, width),
        gk[None], gm[None], gbm, gs[None], gu[None], gd[None], gbs,
    )


def solution(mesh):
    in_specs = (
        P("section", None, ("grp", "walk"), None, None),
        P(None, ("grp", "walk"), None, None),
        P(None, ("grp", "walk"), None, None),
        P("section", "walk", None),
        P("section", None, "walk"),
        P("section", None),
        P("section", "walk", None),
        P("section", "walk", None),
        P("section", "walk", None),
        P("section", None),
        P(),
    )
    out_specs = (
        P("section", None, ("grp", "walk"), None, None),
        P(("grp", "section"), "walk", None),
        P(("grp", "section"), None, "walk"),
        P(("grp", "section"), "walk"),
        P(("grp", "section"), "walk", None),
        P(("grp", "section"), "walk", None),
        P(("grp", "section"), "walk", None),
        P(("grp", "section"), "walk"),
    )
    return jax.shard_map(
        functools.partial(per_device, mesh.shape["walk"], mesh.shape["section"]),
        mesh=mesh, in_specs=in_specs, out_specs=out_specs, check_vma=False,
    )
```

```python
import functools

import jax
import jax.numpy as jnp
from jax import lax
from jax.experimental import pallas as pl
from jax.experimental.pallas import tpu as pltpu
from jax.sharding import PartitionSpec as P

F32 = jnp.float32
BF16 = jnp.bfloat16
MESH = pl.DeviceIdType.MESH


def dot(left, right):
    return jnp.dot(left, right, preferred_element_type=F32)


def dot_tn(left, right):
    return lax.dot_general(left, right, (((0,), (0,)), ((), ())), preferred_element_type=F32)


def dot_nt(left, right):
    return lax.dot_general(left, right, (((1,), (1,)), ((), ())), preferred_element_type=F32)


def join_rows(pieces):
    if pieces[0].shape[0] % 16:
        return jnp.concatenate([piece.astype(F32) for piece in pieces], axis=0).astype(BF16)
    return jnp.concatenate(pieces, axis=0)


def fold(entries):
    while entries.shape[0] > 16:
        half = entries.shape[0] // 2
        entries = entries[:half] + entries[half:]
    return entries


def kernel(
    n_walk, n_section,
    states, pairs_hbm, top, wk, wm, bm, ws, wu, wd, bs, spins,
    dh, total_rest, total_key, total_msg,
    slope, pairs, got_key, got_rest, got_msg, full_w, rhs, onehot, fold_rows, up_rows,
    partial, sums, tz, arrived, dzs, dkeys, ds_up, ds_down, tail, grads,
    out_rest, in_rest, out_key, in_key, out_msg, in_msg,
    pair_sem, w_send, w_recv, p_send, p_recv, g_send, g_recv,
):
    walk = lax.axis_index("walk")
    section = lax.axis_index("section")
    micro, elec, width = states.shape
    pair_width = pairs.shape[1]
    rows = wk.shape[0]
    cols = wm.shape[1]
    scale = 2.0 / elec
    chunk = 8 * elec
    tile = 2 * elec
    chunks = elec // 8

    for w in range(micro):
        pltpu.make_async_copy(pairs_hbm.at[w], pairs.at[w], pair_sem.at[w]).start()

    peers = [lax.rem(walk + step, n_walk) for step in range(1, n_walk)]
    barrier = pltpu.get_barrier_semaphore()
    for peer in peers:
        pl.semaphore_signal(barrier, inc=1, device_id={"walk": peer}, device_id_type=MESH)
    above = lax.rem(section + 1, n_section)
    below = lax.rem(section + n_section - 1, n_section)
    pl.semaphore_signal(barrier, inc=1, device_id={"section": above}, device_id_type=MESH)
    pl.semaphore_signal(barrier, inc=1, device_id={"section": below}, device_id_type=MESH)

    got_key[walk] = wk[...]
    got_rest[walk, 0] = ws[...]
    got_rest[walk, 1] = wu[...]
    got_rest[walk, 2] = wd[...]
    got_msg[walk] = jnp.concatenate([wm[...], jnp.zeros((pair_width, 128 - cols), BF16)], axis=1)

    pl.semaphore_wait(barrier, n_walk + 1)

    def weight_copy(kind, ref, step, slot):
        return pltpu.make_async_remote_copy(
            src_ref=ref.at[slot], dst_ref=ref.at[slot],
            send_sem=w_send.at[kind, step], recv_sem=w_recv.at[kind, slot],
            device_id={"walk": peers[step]}, device_id_type=MESH,
        )

    kinds = ((0, got_key), (1, got_msg), (2, got_rest))
    for kind, ref in kinds:
        for step in range(n_walk - 1):
            weight_copy(kind, ref, step, walk).start()

    q = lax.broadcasted_iota(jnp.int32, (tile, elec), 0)
    j = lax.broadcasted_iota(jnp.int32, (tile, elec), 1)
    onehot[...] = jnp.where(lax.rem(q, elec) == j, 1.0, 0.0).astype(BF16)
    up = jnp.where(spins[...] == 0, 1.0, 0.0)
    r = lax.broadcasted_iota(jnp.int32, fold_rows.shape, 0)
    q = lax.broadcasted_iota(jnp.int32, fold_rows.shape, 1)
    fold_rows[...] = jnp.where(q // 16 == r, 1.0, 0.0).astype(BF16)
    up_column = jnp.transpose(jnp.broadcast_to(up, (elec, elec)))
    up_rows[...] = jnp.concatenate([up_column] * (width // elec), axis=1).astype(BF16)

    @pl.when(section == n_section - 1)
    def _():
        arrived[...] = top[...]

    for kind, ref in kinds[:2]:
        for step in range(n_walk - 1):
            weight_copy(kind, ref, step, peers[step]).wait_recv()
    full_w[0] = join_rows([got_key[k] for k in range(n_walk)])
    w_msg = jnp.concatenate([got_msg[k][:, :cols] for k in range(n_walk)], axis=1)
    for k in range(4):
        before = [jnp.zeros((k * pair_width, width), BF16)] if k else []
        after = [jnp.zeros(((3 - k) * pair_width, width), BF16)] if k < 3 else []
        rhs[k, 0:elec] = jnp.concatenate(before + [w_msg] + after, axis=0)

    def down(w):
        return pltpu.make_async_remote_copy(
            src_ref=dh.at[w], dst_ref=arrived.at[w],
            send_sem=p_send.at[w], recv_sem=p_recv.at[w],
            device_id={"section": below}, device_id_type=MESH,
        )

    def grad_copy(kind, out, into, step, target, slot):
        return pltpu.make_async_remote_copy(
            src_ref=out.at[target], dst_ref=into.at[slot],
            send_sem=g_send.at[kind, step], recv_sem=g_recv.at[kind, slot],
            device_id={"walk": peers[step]}, device_id_type=MESH,
        )

    def begin(w):
        dz = (arrived[w].astype(F32) * tz[w]).astype(BF16)
        dzs[pl.ds(pl.multiple_of(w * elec, elec), elec), :] = dz
        ds_up[...] = dot_nt(dz, full_w[2]) * scale
        ds_down[...] = dot_nt(dz, full_w[3]) * scale

    def finish(w):
        here = pl.ds(pl.multiple_of(w * elec, elec), elec)

        def step(c, carry):
            dkey, grad = carry
            at = pl.ds(pl.multiple_of(c * 8, 8), 8)
            row_up = ds_up[at, :]
            row_down = ds_down[at, :]
            start = pl.multiple_of(c * chunk, chunk)
            parts = []
            for i in range(8):
                one_up = jnp.broadcast_to(row_up[i:i + 1], (elec, width)).astype(BF16)
                one_down = jnp.broadcast_to(row_down[i:i + 1], (elec, width)).astype(BF16)
                spread = jnp.where(up_rows[...] > 0.5, one_up, one_down)
                parts.append(spread * slope[w, pl.ds(start + i * elec, elec), :])
            block = pairs[w, :, pl.ds(start, chunk)]
            for k in range(4):
                both = jnp.concatenate(parts[2 * k:2 * k + 2], axis=0)
                grad = grad + dot(block[:, k * tile:(k + 1) * tile], both)
            while len(parts) > 1:
                parts = [a + b for a, b in zip(parts[::2], parts[1::2])]
            return dkey + parts[0].astype(F32), grad

        dkey, grad = lax.fori_loop(
            0, chunks, step,
            (jnp.zeros((elec, width), F32), jnp.zeros((pair_width, width), F32)), unroll=8,
        )
        dkeys[here, :] = dkey.astype(BF16)
        out = arrived[w].astype(F32) + dot_nt(dzs[here, :], full_w[1])
        dh[w] = (out + dot_nt(dkey.astype(BF16), full_w[0])).astype(BF16)

        @pl.when(section > 0)
        def _():
            down(w).start()

        tail[0:pair_width, :] += grad
        tail[pair_width:pair_width + 1, :] += jnp.sum(dkey, axis=0, keepdims=True)
        tail[pair_width + 1:pair_width + 2, :] += jnp.sum(
            dzs[here, :].astype(F32), axis=0, keepdims=True
        )

    def messages(w, _):
        pltpu.make_async_copy(pairs_hbm.at[w], pairs.at[w], pair_sem.at[w]).wait()
        keyed = (dot(states[w], full_w[0]) + bm[...]).astype(BF16)
        for k in range(4):
            rhs[k, elec:] = keyed

        def step(c, _):
            start = pl.multiple_of(c * chunk, chunk)
            block = pairs[w, :, pl.ds(start, chunk)]
            stacked = jnp.concatenate([block[:, k * tile:(k + 1) * tile] for k in range(4)], axis=0)
            left = jnp.concatenate([jnp.transpose(stacked), onehot[...]], axis=1)
            for k in range(4):
                message = jnp.tanh(dot(left, rhs[k]).astype(BF16))
                slope[w, pl.ds(start + k * tile, tile), :] = 1.0 - message * message
                for i in range(2):
                    one = message[i * elec:(i + 1) * elec]
                    at = pl.ds(pl.multiple_of(c * 128, 128) + (2 * k + i) * 16, 16)
                    partial[0, at, :] = fold(one)
                    partial[1, at, :] = fold(one * up_rows[...])
            return 0

        lax.fori_loop(0, chunks, step, 0, unroll=4)
        at = pl.ds(pl.multiple_of(w * elec, elec), elec)
        sum_both = dot(fold_rows[...], partial[0])
        sum_up = dot(fold_rows[...], partial[1])
        sums[0, at, :] = (sum_up * scale).astype(BF16)
        sums[1, at, :] = ((sum_both - sum_up) * scale).astype(BF16)

        @pl.when(w == 0)
        def _():
            for step in range(n_walk - 1):
                weight_copy(2, got_rest, step, peers[step]).wait_recv()
            for which in range(3):
                full_w[1 + which] = join_rows([got_rest[k, which] for k in range(n_walk)])

        z = dot(states[w], full_w[1]) + dot(sums[0, at, :], full_w[2])
        tanh_z = jnp.tanh(z + dot(sums[1, at, :], full_w[3]) + bs[...])
        tz[w] = 1.0 - tanh_z * tanh_z

        @pl.when(section == n_section - 1)
        def _():
            begin(w)
            finish(w)

        return 0

    tail[...] = jnp.zeros_like(tail)
    lax.fori_loop(0, micro, messages, 0)

    final = micro - 1
    below_top = section < n_section - 1

    @pl.when(below_top)
    def _():
        def walker(w, _):
            down(w).wait_recv()
            begin(w)
            finish(w)
            return 0

        lax.fori_loop(0, final, walker, 0)

    first = slice(0, final * elec)
    last = slice(final * elec, micro * elec)
    h_first = states[0:final].reshape(final * elec, width)
    h_last = states[final]
    grads[0] = dot_tn(h_first, dzs[first, :])
    grads[1] = dot_tn(sums[0, first, :], dzs[first, :])
    grads[2] = dot_tn(sums[1, first, :], dzs[first, :])
    grads[3] = dot_tn(h_first, dkeys[first, :])

    @pl.when(below_top)
    def _():
        down(final).wait_recv()
        begin(final)

    @pl.when(jnp.logical_and(below_top, section > 0))
    def _():
        finish(final)

    lefts = (h_last, sums[0, last, :], sums[1, last, :])
    for which in range(3):
        grad = grads[which] + dot_tn(lefts[which], dzs[last, :])
        for k in range(n_walk):
            out_rest[k, which] = grad[k * rows:(k + 1) * rows].astype(BF16)
    for step in range(n_walk - 1):
        grad_copy(0, out_rest, in_rest, step, peers[step], walk).start()

    @pl.when(section == 0)
    def _():
        finish(final)

    grad = grads[3] + dot_tn(h_last, dkeys[last, :])
    for k in range(n_walk):
        out_key[k] = grad[k * rows:(k + 1) * rows].astype(BF16)
        part = tail[...][:, k * cols:(k + 1) * cols]
        out_msg[k] = jnp.concatenate(
            [part, jnp.zeros((tail.shape[0], 128 - cols), F32)], axis=1
        ).astype(BF16)
    for step in range(n_walk - 1):
        grad_copy(1, out_key, in_key, step, peers[step], walk).start()
        grad_copy(2, out_msg, in_msg, step, peers[step], walk).start()

    def collect(kind, out, into):
        total = out[walk].astype(F32)
        for step in range(n_walk - 1):
            grad_copy(kind, out, into, step, peers[step], peers[step]).wait_recv()
            total = total + into[peers[step]].astype(F32)
        return total * (1.0 / elec)

    total_rest[...] = collect(0, out_rest, in_rest)
    total_key[...] = collect(1, out_key, in_key)
    total_msg[...] = collect(2, out_msg, in_msg)

    for kind, ref in kinds:
        for step in range(n_walk - 1):
            weight_copy(kind, ref, step, walk).wait_send()
    for kind, out, into in ((0, out_rest, in_rest), (1, out_key, in_key), (2, out_msg, in_msg)):
        for step in range(n_walk - 1):
            grad_copy(kind, out, into, step, peers[step], walk).wait_send()

    @pl.when(section > 0)
    def _():
        for w in range(micro):
            down(w).wait_send()


def spread_out(
    dh_in, total_rest, total_key, total_msg, dh, gk, gm, gbm, gs, gu, gd, gbs
):
    pair_width, cols = gm.shape
    dh[...] = dh_in[...]
    gk[...] = total_key[...]
    gs[...] = total_rest[0]
    gu[...] = total_rest[1]
    gd[...] = total_rest[2]
    gm[...] = total_msg[:pair_width, :cols]
    gbm[...] = total_msg[pair_width:pair_width + 1, :cols]
    gbs[...] = total_msg[pair_width + 1:pair_width + 2, :cols]


def per_device(
    n_walk, n_section,
    states, pair_feats, top_cotangent, w_key, w_msg, b_msg, w_self, w_up, w_down, b_self, spins
):
    micro, walkers, elec, width = states.shape[1:]
    pair_width = pair_feats.shape[2]
    count = micro * walkers
    rows = w_key.shape[1]
    cols = w_msg.shape[2]
    tail = pair_width + 16
    vmem = pl.BlockSpec(memory_space=pltpu.VMEM)
    shape = jax.ShapeDtypeStruct
    raw = pl.pallas_call(
        functools.partial(kernel, n_walk, n_section),
        out_shape=(
            shape((count, elec, width), BF16),
            shape((3, rows, width), F32),
            shape((rows, width), F32),
            shape((tail, 128), F32),
        ),
        in_specs=[vmem, pl.BlockSpec(memory_space=pl.ANY)] + [vmem] * 9,
        out_specs=(vmem,) * 4,
        scratch_shapes=[
            pltpu.VMEM((count, elec * elec, width), BF16),
            pltpu.VMEM((count, pair_width, elec * elec), BF16),
            pltpu.VMEM((n_walk, rows, width), BF16),
            pltpu.VMEM((n_walk, 3, rows, width), BF16),
            pltpu.VMEM((n_walk, pair_width, 128), BF16),
            pltpu.VMEM((4, width, width), BF16),
            pltpu.VMEM((4, 2 * elec, width), BF16),
            pltpu.VMEM((2 * elec, elec), BF16),
            pltpu.VMEM((elec, 16 * elec), BF16),
            pltpu.VMEM((elec, width), BF16),
            pltpu.VMEM((2, 16 * elec, width), BF16),
            pltpu.VMEM((2, count * elec, width), BF16),
            pltpu.VMEM((count, elec, width), F32),
            pltpu.VMEM((count, elec, width), BF16),
            pltpu.VMEM((count * elec, width), BF16),
            pltpu.VMEM((count * elec, width), BF16),
            pltpu.VMEM((elec, width), F32),
            pltpu.VMEM((elec, width), F32),
            pltpu.VMEM((tail, width), F32),
            pltpu.VMEM((4, width, width), F32),
            pltpu.VMEM((n_walk, 3, rows, width), BF16),
            pltpu.VMEM((n_walk, 3, rows, width), BF16),
            pltpu.VMEM((n_walk, rows, width), BF16),
            pltpu.VMEM((n_walk, rows, width), BF16),
            pltpu.VMEM((n_walk, tail, 128), BF16),
            pltpu.VMEM((n_walk, tail, 128), BF16),
            pltpu.SemaphoreType.DMA((count,)),
            pltpu.SemaphoreType.DMA((3, n_walk)),
            pltpu.SemaphoreType.DMA((3, n_walk)),
            pltpu.SemaphoreType.DMA((count,)),
            pltpu.SemaphoreType.DMA((count,)),
            pltpu.SemaphoreType.DMA((3, n_walk)),
            pltpu.SemaphoreType.DMA((3, n_walk)),
        ],
        compiler_params=pltpu.CompilerParams(
            collective_id=0, has_side_effects=True, vmem_limit_bytes=58 * 1024 * 1024
        ),
    )(
        states[0].reshape(count, elec, width),
        pair_feats.reshape(count, pair_width, elec * elec),
        top_cotangent.reshape(count, elec, width),
        w_key[0], w_msg[0], b_msg, w_self[0], w_up[0], w_down[0], b_self,
        spins.reshape(1, elec),
    )
    dh, gk, gm, gbm, gs, gu, gd, gbs = pl.pallas_call(
        spread_out,
        out_shape=(
            shape((count, elec, width), BF16),
            shape((rows, width), F32),
            shape((pair_width, cols), F32),
            shape((1, cols), F32),
            shape((rows, width), F32),
            shape((rows, width), F32),
            shape((rows, width), F32),
            shape((1, cols), F32),
        ),
        in_specs=[vmem] * 4,
        out_specs=(vmem,) * 8,
    )(*raw)
    return (
        dh.reshape(1, micro, walkers, elec, width),
        gk[None], gm[None], gbm, gs[None], gu[None], gd[None], gbs,
    )


def solution(mesh):
    in_specs = (
        P("section", None, ("grp", "walk"), None, None),
        P(None, ("grp", "walk"), None, None),
        P(None, ("grp", "walk"), None, None),
        P("section", "walk", None),
        P("section", None, "walk"),
        P("section", None),
        P("section", "walk", None),
        P("section", "walk", None),
        P("section", "walk", None),
        P("section", None),
        P(),
    )
    out_specs = (
        P("section", None, ("grp", "walk"), None, None),
        P(("grp", "section"), "walk", None),
        P(("grp", "section"), None, "walk"),
        P(("grp", "section"), "walk"),
        P(("grp", "section"), "walk", None),
        P(("grp", "section"), "walk", None),
        P(("grp", "section"), "walk", None),
        P(("grp", "section"), "walk"),
    )
    return jax.shard_map(
        functools.partial(per_device, mesh.shape["walk"], mesh.shape["section"]),
        mesh=mesh, in_specs=in_specs, out_specs=out_specs, check_vma=False,
    )
```

```python
import functools

import jax
import jax.numpy as jnp
from jax import lax
from jax.experimental import pallas as pl
from jax.experimental.pallas import tpu as pltpu
from jax.sharding import PartitionSpec as P

F32 = jnp.float32
BF16 = jnp.bfloat16
MESH = pl.DeviceIdType.MESH


def dot(left, right):
    return jnp.dot(left, right, preferred_element_type=F32)


def dot_tn(left, right):
    return lax.dot_general(left, right, (((0,), (0,)), ((), ())), preferred_element_type=F32)


def dot_nt(left, right):
    return lax.dot_general(left, right, (((1,), (1,)), ((), ())), preferred_element_type=F32)


def join_rows(pieces):
    if pieces[0].shape[0] % 16:
        return jnp.concatenate([piece.astype(F32) for piece in pieces], axis=0).astype(BF16)
    return jnp.concatenate(pieces, axis=0)


def fold(entries):
    while entries.shape[0] > 16:
        half = entries.shape[0] // 2
        entries = entries[:half] + entries[half:]
    return entries


def kernel(
    n_walk, n_section,
    states, pairs_hbm, top, wk, wm, bm, ws, wu, wd, bs, spins,
    dh, total_rest, total_key, total_msg,
    slope, pairs, got_key, got_rest, got_msg, full_w, rhs, onehot, fold_rows, up_rows,
    partial, sums, tz, arrived, dzs, dkeys, ds_up, ds_down, tail, grads,
    out_rest, in_rest, out_key, in_key, out_msg, in_msg,
    pair_sem, w_send, w_recv, p_send, p_recv, g_send, g_recv,
):
    walk = lax.axis_index("walk")
    section = lax.axis_index("section")
    micro, elec, width = states.shape
    pair_width = pairs.shape[1]
    rows = wk.shape[0]
    cols = wm.shape[1]
    scale = 2.0 / elec
    chunk = 8 * elec
    tile = 2 * elec
    chunks = elec // 8

    for w in range(micro):
        pltpu.make_async_copy(pairs_hbm.at[w], pairs.at[w], pair_sem.at[w]).start()

    peers = [lax.rem(walk + step, n_walk) for step in range(1, n_walk)]
    barrier = pltpu.get_barrier_semaphore()
    for peer in peers:
        pl.semaphore_signal(barrier, inc=1, device_id={"walk": peer}, device_id_type=MESH)
    above = lax.rem(section + 1, n_section)
    below = lax.rem(section + n_section - 1, n_section)
    pl.semaphore_signal(barrier, inc=1, device_id={"section": above}, device_id_type=MESH)
    pl.semaphore_signal(barrier, inc=1, device_id={"section": below}, device_id_type=MESH)

    got_key[walk] = wk[...]
    got_rest[walk, 0] = ws[...]
    got_rest[walk, 1] = wu[...]
    got_rest[walk, 2] = wd[...]
    got_msg[walk] = jnp.concatenate([wm[...], jnp.zeros((pair_width, 128 - cols), BF16)], axis=1)

    pl.semaphore_wait(barrier, n_walk + 1)

    def weight_copy(kind, ref, step, slot):
        return pltpu.make_async_remote_copy(
            src_ref=ref.at[slot], dst_ref=ref.at[slot],
            send_sem=w_send.at[kind, step], recv_sem=w_recv.at[kind, slot],
            device_id={"walk": peers[step]}, device_id_type=MESH,
        )

    kinds = ((0, got_key), (1, got_msg), (2, got_rest))
    for kind, ref in kinds:
        for step in range(n_walk - 1):
            weight_copy(kind, ref, step, walk).start()

    q = lax.broadcasted_iota(jnp.int32, (tile, elec), 0)
    j = lax.broadcasted_iota(jnp.int32, (tile, elec), 1)
    onehot[...] = jnp.where(lax.rem(q, elec) == j, 1.0, 0.0).astype(BF16)
    up = jnp.where(spins[...] == 0, 1.0, 0.0)
    r = lax.broadcasted_iota(jnp.int32, fold_rows.shape, 0)
    q = lax.broadcasted_iota(jnp.int32, fold_rows.shape, 1)
    fold_rows[...] = jnp.where(q // 16 == r, 1.0, 0.0).astype(BF16)
    up_column = jnp.transpose(jnp.broadcast_to(up, (elec, elec)))
    up_rows[...] = jnp.concatenate([up_column] * (width // elec), axis=1).astype(BF16)

    @pl.when(section == n_section - 1)
    def _():
        arrived[...] = top[...]

    for kind, ref in kinds[:2]:
        for step in range(n_walk - 1):
            weight_copy(kind, ref, step, peers[step]).wait_recv()
    full_w[0] = join_rows([got_key[k] for k in range(n_walk)])
    w_msg = jnp.concatenate([got_msg[k][:, :cols] for k in range(n_walk)], axis=1)
    for k in range(4):
        before = [jnp.zeros((k * pair_width, width), BF16)] if k else []
        after = [jnp.zeros(((3 - k) * pair_width, width), BF16)] if k < 3 else []
        rhs[k, 0:elec] = jnp.concatenate(before + [w_msg] + after, axis=0)

    def down(w):
        return pltpu.make_async_remote_copy(
            src_ref=dh.at[w], dst_ref=arrived.at[w],
            send_sem=p_send.at[w], recv_sem=p_recv.at[w],
            device_id={"section": below}, device_id_type=MESH,
        )

    def grad_copy(kind, out, into, step, target, slot):
        return pltpu.make_async_remote_copy(
            src_ref=out.at[target], dst_ref=into.at[slot],
            send_sem=g_send.at[kind, step], recv_sem=g_recv.at[kind, slot],
            device_id={"walk": peers[step]}, device_id_type=MESH,
        )

    def rows_of(w):
        return pl.ds(w * elec if isinstance(w, int) else pl.multiple_of(w * elec, elec), elec)

    def begin(w):
        dz = (arrived[w].astype(F32) * tz[w]).astype(BF16)
        dzs[rows_of(w), :] = dz
        ds_up[...] = dot_nt(dz, full_w[2]) * scale
        ds_down[...] = dot_nt(dz, full_w[3]) * scale

    def finish(w):
        here = rows_of(w)

        def step(c, carry):
            dkey, grad = carry
            at = pl.ds(pl.multiple_of(c * 8, 8), 8)
            row_up = ds_up[at, :]
            row_down = ds_down[at, :]
            start = pl.multiple_of(c * chunk, chunk)
            parts = []
            for i in range(8):
                one_up = jnp.broadcast_to(row_up[i:i + 1], (elec, width)).astype(BF16)
                one_down = jnp.broadcast_to(row_down[i:i + 1], (elec, width)).astype(BF16)
                spread = jnp.where(up_rows[...] > 0.5, one_up, one_down)
                parts.append(spread * slope[w, pl.ds(start + i * elec, elec), :])
            block = pairs[w, :, pl.ds(start, chunk)]
            for k in range(4):
                both = jnp.concatenate(parts[2 * k:2 * k + 2], axis=0)
                grad = grad + dot(block[:, k * tile:(k + 1) * tile], both)
            while len(parts) > 1:
                parts = [a + b for a, b in zip(parts[::2], parts[1::2])]
            return dkey + parts[0].astype(F32), grad

        dkey, grad = lax.fori_loop(
            0, chunks, step,
            (jnp.zeros((elec, width), F32), jnp.zeros((pair_width, width), F32)), unroll=8,
        )
        dkeys[here, :] = dkey.astype(BF16)
        out = arrived[w].astype(F32) + dot_nt(dzs[here, :], full_w[1])
        dh[w] = (out + dot_nt(dkey.astype(BF16), full_w[0])).astype(BF16)

        @pl.when(section > 0)
        def _():
            down(w).start()

        tail[0:pair_width, :] += grad
        tail[pair_width:pair_width + 1, :] += jnp.sum(dkey, axis=0, keepdims=True)
        tail[pair_width + 1:pair_width + 2, :] += jnp.sum(
            dzs[here, :].astype(F32), axis=0, keepdims=True
        )

    def messages(w, _):
        pltpu.make_async_copy(pairs_hbm.at[w], pairs.at[w], pair_sem.at[w]).wait()
        keyed = (dot(states[w], full_w[0]) + bm[...]).astype(BF16)
        for k in range(4):
            rhs[k, elec:] = keyed

        def step(c, _):
            start = pl.multiple_of(c * chunk, chunk)
            block = pairs[w, :, pl.ds(start, chunk)]
            stacked = jnp.concatenate([block[:, k * tile:(k + 1) * tile] for k in range(4)], axis=0)
            left = jnp.concatenate([jnp.transpose(stacked), onehot[...]], axis=1)
            for k in range(4):
                message = jnp.tanh(dot(left, rhs[k]).astype(BF16))
                slope[w, pl.ds(start + k * tile, tile), :] = 1.0 - message * message
                for i in range(2):
                    one = message[i * elec:(i + 1) * elec]
                    at = pl.ds(pl.multiple_of(c * 128, 128) + (2 * k + i) * 16, 16)
                    partial[0, at, :] = fold(one)
                    partial[1, at, :] = fold(one * up_rows[...])
            return 0

        lax.fori_loop(0, chunks, step, 0, unroll=4)
        at = rows_of(w)
        sum_both = dot(fold_rows[...], partial[0])
        sum_up = dot(fold_rows[...], partial[1])
        sums[0, at, :] = (sum_up * scale).astype(BF16)
        sums[1, at, :] = ((sum_both - sum_up) * scale).astype(BF16)

        @pl.when(w == 1)
        def _():
            for step in range(n_walk - 1):
                weight_copy(2, got_rest, step, peers[step]).wait_recv()
            for which in range(3):
                full_w[1 + which] = join_rows([got_rest[k, which] for k in range(n_walk)])

        @pl.when(w > 0)
        def _():
            settle(w - 1)

        return 0

    def settle(w):
        at = rows_of(w)
        z = dot(states[w], full_w[1]) + dot(sums[0, at, :], full_w[2])
        tanh_z = jnp.tanh(z + dot(sums[1, at, :], full_w[3]) + bs[...])
        tz[w] = 1.0 - tanh_z * tanh_z

        @pl.when(section == n_section - 1)
        def _():
            begin(w)
            finish(w)

    tail[...] = jnp.zeros_like(tail)
    lax.fori_loop(0, micro, messages, 0)
    settle(micro - 1)

    final = micro - 1
    below_top = section < n_section - 1

    @pl.when(below_top)
    def _():
        def walker(w, _):
            down(w).wait_recv()
            begin(w)
            finish(w)
            return 0

        lax.fori_loop(0, final, walker, 0)

    first = slice(0, final * elec)
    last = slice(final * elec, micro * elec)
    h_first = states[0:final].reshape(final * elec, width)
    h_last = states[final]
    grads[0] = dot_tn(h_first, dzs[first, :])
    grads[1] = dot_tn(sums[0, first, :], dzs[first, :])
    grads[2] = dot_tn(sums[1, first, :], dzs[first, :])
    grads[3] = dot_tn(h_first, dkeys[first, :])

    @pl.when(below_top)
    def _():
        down(final).wait_recv()
        begin(final)

    @pl.when(jnp.logical_and(below_top, section > 0))
    def _():
        finish(final)

    lefts = (h_last, sums[0, last, :], sums[1, last, :])
    for which in range(3):
        grad = grads[which] + dot_tn(lefts[which], dzs[last, :])
        for k in range(n_walk):
            out_rest[k, which] = grad[k * rows:(k + 1) * rows].astype(BF16)
    for step in range(n_walk - 1):
        grad_copy(0, out_rest, in_rest, step, peers[step], walk).start()

    @pl.when(section == 0)
    def _():
        finish(final)

    grad = grads[3] + dot_tn(h_last, dkeys[last, :])
    for k in range(n_walk):
        out_key[k] = grad[k * rows:(k + 1) * rows].astype(BF16)
        part = tail[...][:, k * cols:(k + 1) * cols]
        out_msg[k] = jnp.concatenate(
            [part, jnp.zeros((tail.shape[0], 128 - cols), F32)], axis=1
        ).astype(BF16)
    for step in range(n_walk - 1):
        grad_copy(1, out_key, in_key, step, peers[step], walk).start()
        grad_copy(2, out_msg, in_msg, step, peers[step], walk).start()

    def collect(kind, out, into):
        total = out[walk].astype(F32)
        for step in range(n_walk - 1):
            grad_copy(kind, out, into, step, peers[step], peers[step]).wait_recv()
            total = total + into[peers[step]].astype(F32)
        return total * (1.0 / elec)

    total_rest[...] = collect(0, out_rest, in_rest)
    total_key[...] = collect(1, out_key, in_key)
    total_msg[...] = collect(2, out_msg, in_msg)

    for kind, ref in kinds:
        for step in range(n_walk - 1):
            weight_copy(kind, ref, step, walk).wait_send()
    for kind, out, into in ((0, out_rest, in_rest), (1, out_key, in_key), (2, out_msg, in_msg)):
        for step in range(n_walk - 1):
            grad_copy(kind, out, into, step, peers[step], walk).wait_send()

    @pl.when(section > 0)
    def _():
        for w in range(micro):
            down(w).wait_send()


def spread_out(
    dh_in, total_rest, total_key, total_msg, dh, gk, gm, gbm, gs, gu, gd, gbs
):
    pair_width, cols = gm.shape
    dh[...] = dh_in[...]
    gk[...] = total_key[...]
    gs[...] = total_rest[0]
    gu[...] = total_rest[1]
    gd[...] = total_rest[2]
    gm[...] = total_msg[:pair_width, :cols]
    gbm[...] = total_msg[pair_width:pair_width + 1, :cols]
    gbs[...] = total_msg[pair_width + 1:pair_width + 2, :cols]


def per_device(
    n_walk, n_section,
    states, pair_feats, top_cotangent, w_key, w_msg, b_msg, w_self, w_up, w_down, b_self, spins
):
    micro, walkers, elec, width = states.shape[1:]
    pair_width = pair_feats.shape[2]
    count = micro * walkers
    rows = w_key.shape[1]
    cols = w_msg.shape[2]
    tail = pair_width + 16
    vmem = pl.BlockSpec(memory_space=pltpu.VMEM)
    shape = jax.ShapeDtypeStruct
    raw = pl.pallas_call(
        functools.partial(kernel, n_walk, n_section),
        out_shape=(
            shape((count, elec, width), BF16),
            shape((3, rows, width), F32),
            shape((rows, width), F32),
            shape((tail, 128), F32),
        ),
        in_specs=[vmem, pl.BlockSpec(memory_space=pl.ANY)] + [vmem] * 9,
        out_specs=(vmem,) * 4,
        scratch_shapes=[
            pltpu.VMEM((count, elec * elec, width), BF16),
            pltpu.VMEM((count, pair_width, elec * elec), BF16),
            pltpu.VMEM((n_walk, rows, width), BF16),
            pltpu.VMEM((n_walk, 3, rows, width), BF16),
            pltpu.VMEM((n_walk, pair_width, 128), BF16),
            pltpu.VMEM((4, width, width), BF16),
            pltpu.VMEM((4, 2 * elec, width), BF16),
            pltpu.VMEM((2 * elec, elec), BF16),
            pltpu.VMEM((elec, 16 * elec), BF16),
            pltpu.VMEM((elec, width), BF16),
            pltpu.VMEM((2, 16 * elec, width), BF16),
            pltpu.VMEM((2, count * elec, width), BF16),
            pltpu.VMEM((count, elec, width), F32),
            pltpu.VMEM((count, elec, width), BF16),
            pltpu.VMEM((count * elec, width), BF16),
            pltpu.VMEM((count * elec, width), BF16),
            pltpu.VMEM((elec, width), F32),
            pltpu.VMEM((elec, width), F32),
            pltpu.VMEM((tail, width), F32),
            pltpu.VMEM((4, width, width), F32),
            pltpu.VMEM((n_walk, 3, rows, width), BF16),
            pltpu.VMEM((n_walk, 3, rows, width), BF16),
            pltpu.VMEM((n_walk, rows, width), BF16),
            pltpu.VMEM((n_walk, rows, width), BF16),
            pltpu.VMEM((n_walk, tail, 128), BF16),
            pltpu.VMEM((n_walk, tail, 128), BF16),
            pltpu.SemaphoreType.DMA((count,)),
            pltpu.SemaphoreType.DMA((3, n_walk)),
            pltpu.SemaphoreType.DMA((3, n_walk)),
            pltpu.SemaphoreType.DMA((count,)),
            pltpu.SemaphoreType.DMA((count,)),
            pltpu.SemaphoreType.DMA((3, n_walk)),
            pltpu.SemaphoreType.DMA((3, n_walk)),
        ],
        compiler_params=pltpu.CompilerParams(
            collective_id=0, has_side_effects=True, vmem_limit_bytes=58 * 1024 * 1024
        ),
    )(
        states[0].reshape(count, elec, width),
        pair_feats.reshape(count, pair_width, elec * elec),
        top_cotangent.reshape(count, elec, width),
        w_key[0], w_msg[0], b_msg, w_self[0], w_up[0], w_down[0], b_self,
        spins.reshape(1, elec),
    )
    dh, gk, gm, gbm, gs, gu, gd, gbs = pl.pallas_call(
        spread_out,
        out_shape=(
            shape((count, elec, width), BF16),
            shape((rows, width), F32),
            shape((pair_width, cols), F32),
            shape((1, cols), F32),
            shape((rows, width), F32),
            shape((rows, width), F32),
            shape((rows, width), F32),
            shape((1, cols), F32),
        ),
        in_specs=[vmem] * 4,
        out_specs=(vmem,) * 8,
    )(*raw)
    return (
        dh.reshape(1, micro, walkers, elec, width),
        gk[None], gm[None], gbm, gs[None], gu[None], gd[None], gbs,
    )


def solution(mesh):
    in_specs = (
        P("section", None, ("grp", "walk"), None, None),
        P(None, ("grp", "walk"), None, None),
        P(None, ("grp", "walk"), None, None),
        P("section", "walk", None),
        P("section", None, "walk"),
        P("section", None),
        P("section", "walk", None),
        P("section", "walk", None),
        P("section", "walk", None),
        P("section", None),
        P(),
    )
    out_specs = (
        P("section", None, ("grp", "walk"), None, None),
        P(("grp", "section"), "walk", None),
        P(("grp", "section"), None, "walk"),
        P(("grp", "section"), "walk"),
        P(("grp", "section"), "walk", None),
        P(("grp", "section"), "walk", None),
        P(("grp", "section"), "walk", None),
        P(("grp", "section"), "walk"),
    )
    return jax.shard_map(
        functools.partial(per_device, mesh.shape["walk"], mesh.shape["section"]),
        mesh=mesh, in_specs=in_specs, out_specs=out_specs, check_vma=False,
    )
```
